512 devices in a mesh: expert: 32 (over y, z_lo, core), dp: 16 (over z_hi, x).
Axes of the slice: x: 4, y: 4, z: 16 (z_hi: 4, z_lo: 4; z = z_hi * 4 + z_lo), core: 2. Of those that a mesh axis runs over, the one named last changes fastest.
Arguments:
- hidden_acts: bfloat16 [4096, 4, 1024], P('expert', None, 'dp'), may hold values from -6 to 6
- expert_ids: int32 [4096, 4], P('expert'), may hold values from 0 to 31, all different within a row; in each aligned block of 128 rows (0 to 127, 128 to 255, ...) at most 32 rows name the same one
- gate_weights: float32 [4096, 4], P('expert'), may hold values from 0.05 to 0.6
- cotangent: bfloat16 [4096, 3584], P('expert', 'dp'), may hold values from -6 to 6
- weight_old: bfloat16 [32, 4864, 1024], P('expert', 'dp'), may hold values from -0.1875 to 0.1875
- first_old: bfloat16 [32, 4864, 1024], P('expert', 'dp'), may hold values from -30 to 30
- second_old: bfloat16 [32, 4864, 1024], P('expert', 'dp'), may hold values from 20 to 400
- old_place: int32 [3584], replicated, may hold values from 0 to 3647, as said below
- new_place: int32 [3584], replicated, may hold values from 0 to 3583, as said below
Outputs:
- combined: bfloat16 [4096, 3584], P('expert', 'dp')
- weight_new: bfloat16 [32, 3584, 1024], P('expert', 'dp')
- first_new: bfloat16 [32, 3584, 1024], P('expert', 'dp')
- second_new: bfloat16 [32, 3584, 1024], P('expert', 'dp')
The draws below stay inside these ranges and needn't reach their ends.
Inputs may be any that keep to these rules, and one draw needn't show every extreme that they name: `expert_ids`: within the rows of one device each expert is named by at most 32 slots, a bound that some block reaches; the slots of one token name distinct experts. `new_place`: each new slot once. New slot q lies on dp device q // 224. `old_place`: distinct old slots. Old slot p lies on dp device p // 304, which is below 12. Of the rows that one old device holds, at most 19 go to any one new device, and exactly 19 for some pair of devices.
All inputs are finite; a program needn't handle non-finite values.
Results may differ from the reference program's by a relative error of at most 0.0049.
Values may be sent and summed in bfloat16 or wider, within the bound.
No kernel may reach another device: no remote copies, remote signals or barrier semaphores. Data moves between devices by JAX's collectives and lax.ppermute only.
A program may use at most 64 MiB of HBM per device.

```python
import math
import jax
import jax.numpy as jnp
import numpy as np
from jax import lax

D = 3584
FF = 1024
TOP = 4
TOK_DEV = 128
TOKENS = 4096
EXPERTS = 32
CAP = 32
OLD_ROWS = 304
N_EXPERT = 32
N_DP = 16


def layout_tables(seed_key):
    old_group = 3 * N_DP // 4
    slice_width = D // N_DP
    key_perm, key_rot, key_pos = jax.random.split(seed_key, 3)
    new_place = jax.random.permutation(key_perm, D).astype(jnp.int32)
    slot_index = jnp.arange(D, dtype=jnp.int32)
    rotation = jax.random.randint(key_rot, (N_DP,), 0, old_group).astype(jnp.int32)
    old_owner = (slot_index % slice_width + rotation[slot_index // slice_width]) % old_group
    owner_hot = (old_owner[:, None] == jnp.arange(old_group, dtype=jnp.int32)[None, :]).astype(jnp.int32)
    arrival = jnp.sum((jnp.cumsum(owner_hot, axis=0) - owner_hot) * owner_hot, axis=1)
    shuffle = jax.random.permutation(key_pos, OLD_ROWS).astype(jnp.int32)
    position = jnp.where(old_owner == 0, arrival, jnp.where(old_owner == old_group - 1, OLD_ROWS - 1 - arrival, shuffle[arrival]))
    old_of_slot = old_owner * OLD_ROWS + position
    old_place = jnp.take(old_of_slot, new_place)
    return (old_place, new_place)


def draw_old_place(key, part):
    tables = layout_tables(key)
    return tables[0].astype(jnp.int32)


def draw_new_place(key, part):
    tables = layout_tables(key)
    return tables[1].astype(jnp.int32)


def shard_levels(rng, dims, pieces, low, largest):
    loudness, own = 1.0, jax.random.fold_in(rng, 6)
    for dim, parts in pieces:
        heights = jnp.exp(jax.random.uniform(jax.random.fold_in(own, dim), (parts,), jnp.float32, low / len(pieces), largest / len(pieces)))
        loudness = loudness * jnp.repeat(heights, dims[dim] // parts).reshape([-1 if axis == dim else 1 for axis in range(len(dims))])
    return loudness


def shared_out(rng, own, number, rows, amount, top, reach, lean):
    order = jax.random.permutation(rng, amount)
    packed, common = portions_of(amount, rows * top, reach, lean, True), portions_of(amount, rows * top, reach, lean, False)
    places = jnp.arange(amount)

    def named(sizes, turn):
        used = int((sizes > 0).sum())
        fixed = max(1, used // 4)
        passed = fixed + (places - fixed + turn * (used - fixed)) % max(1, amount - fixed)
        return jnp.zeros((amount,), jnp.int32).at[order[jnp.where(places < fixed, places, passed)]].set(jnp.asarray(sizes, jnp.int32))

    sizes = jnp.where(number % 4 == 0, named(packed, number // 4), named(common, number - number // 4 - 1))
    mixed = jax.random.permutation(jax.random.fold_in(own, 3), amount)
    giver, taker = mixed[0:amount // 2 * 2:2], mixed[1:amount // 2 * 2:2]
    room = jnp.minimum(sizes[giver] - 1, reach - sizes[taker]) // 2
    room = jnp.where((giver == order[0]) | (taker == order[0]) | (sizes[taker] == 0), 0, jnp.maximum(room, 0))
    passed = jax.random.randint(jax.random.fold_in(own, 4), (amount // 2,), 0, 1 << 20) % (room + 1)
    sizes = sizes.at[giver].add(-passed).at[taker].add(passed)
    items = jnp.searchsorted(jnp.cumsum(sizes), jnp.arange(rows * top), side="right").astype(jnp.int32)
    listing = items.reshape(top, rows).T
    listing = listing[jax.random.permutation(jax.random.fold_in(own, 1), rows)]
    turn = jax.random.randint(jax.random.fold_in(own, 2), (rows, 1), 0, top)
    return jnp.take_along_axis(listing, (jnp.arange(top)[None, :] + turn) % top, axis=1)


def portions_of(number_of, total, reach, lean, full):
    portions = [(1 << 20) // math.isqrt(grade ** lean) + 1 for grade in range(1, number_of + 1)]
    largest = reach if full else min(reach, max(-(-total // number_of), total * portions[0] // sum(portions)))
    least = 1 if total - largest >= number_of - 1 else 0
    given, rest = [largest] + [least] * (number_of - 1), total - largest - least * (number_of - 1)
    while rest > 0:
        free = [i for i in range(1, number_of) if given[i] < largest] or [i for i in range(1, number_of) if given[i] < reach]
        pool, remaining = sum([portions[i] for i in free]), rest
        for i in free:
            extra = min(reach - given[i], max(1, remaining * portions[i] // pool), rest)
            given[i] = given[i] + extra
            rest = rest - extra
    return np.array(given)


def scatter_about(own_key, dims, deviation, reach, shards=(), held_as=jnp.bfloat16):
    values = deviation * jax.random.normal(own_key, dims, jnp.float32)
    if shards:
        values = values * shard_levels(own_key, dims, shards, -0.22, 0.18)
    return jnp.clip(values, -reach, reach).astype(held_as)


def setup_inputs(seed: int = 0) -> dict:
    splits = jax.random.split(jax.random.key(seed), 10)
    hidden_acts = scatter_about(splits[0], (TOKENS, TOP, FF), 1.0, 6.0, ((0, 32), (2, 16)))
    expert_ids_keys = jax.random.split(jax.random.fold_in(splits[1], 1), TOKENS // TOK_DEV)
    expert_ids_turns = jax.random.permutation(jax.random.fold_in(splits[1], 3), TOKENS // TOK_DEV)
    expert_ids = jax.vmap(lambda own, number: shared_out(jax.random.fold_in(splits[1], 2), own, number, TOK_DEV, EXPERTS, TOP, CAP, 2))(expert_ids_keys, expert_ids_turns).reshape((TOKENS, TOP))
    gate_weights = jnp.clip(0.05 + 0.55 * jax.random.uniform(splits[2], (TOKENS, TOP), jnp.float32) ** shard_levels(splits[2], (TOKENS, TOP), ((0, 32),), -0.2, 0.2), 0.05, 0.6)
    cotangent = scatter_about(splits[3], (TOKENS, D), 1.0, 6.0, ((0, 32), (1, 16)))
    weight_old = scatter_about(splits[4], (EXPERTS, N_DP * OLD_ROWS, FF), FF ** -0.5, 0.1875, ((0, 32), (1, 16)))
    first_old = scatter_about(splits[5], (EXPERTS, N_DP * OLD_ROWS, FF), 5.0, 30.0, ((0, 32), (1, 16)))
    second_old = jnp.clip(jnp.exp(math.log(400.0) - 2.9957323 * jax.random.uniform(splits[6], (EXPERTS, N_DP * OLD_ROWS, FF), jnp.float32) ** shard_levels(splits[6], (EXPERTS, N_DP * OLD_ROWS, FF), ((0, 32), (1, 16)), -0.2, 0.2)), 20.0, 400.0).astype(jnp.bfloat16)
    old_place = draw_old_place(jax.random.fold_in(splits[9], 71), 0)
    new_place = draw_new_place(jax.random.fold_in(splits[9], 71), 0)
    return dict(hidden_acts=hidden_acts, expert_ids=expert_ids, gate_weights=gate_weights, cotangent=cotangent, weight_old=weight_old, first_old=first_old, second_old=second_old, old_place=old_place, new_place=new_place)


beta_one = 0.9
beta_two = 0.95
adam_eps = 1e-08
learn_rate = 0.001
weight_decay = 0.1
bias_one = 1.0 - 0.9 ** 50 * 0.9 ** 50
bias_two = 1.0 - 0.95 ** 50 * 0.95 ** 50

def adamw_step(weight, moment_one, second, gradient):
    weight_wide = weight.astype(jnp.float32)
    one_next = beta_one * moment_one.astype(jnp.float32) + (1.0 - beta_one) * gradient
    two_next = beta_two * second.astype(jnp.float32) + (1.0 - beta_two) * gradient * gradient
    update = one_next / bias_one / (jnp.sqrt(two_next / bias_two) + adam_eps) + weight_decay * weight_wide
    return ((weight_wide - learn_rate * update).astype(jnp.bfloat16), one_next.astype(jnp.bfloat16), two_next.astype(jnp.bfloat16))

def reference(hidden_acts, expert_ids, gate_weights, cotangent, weight_old, first_old, second_old, old_place, new_place):
    tokens, top_count, hidden = hidden_acts.shape
    model_width = cotangent.shape[1]
    slot_count = tokens * top_count
    most_rows = N_EXPERT * CAP
    flat_ids = expert_ids.reshape(slot_count)
    flat_gates = jnp.concatenate([gate_weights.reshape(slot_count), jnp.zeros((1,), gate_weights.dtype)])
    acts_pad = jnp.concatenate([hidden_acts.reshape(slot_count, hidden), jnp.zeros((1, hidden), hidden_acts.dtype)], axis=0)
    scaled = (gate_weights[:, :, None] * cotangent[:, None, :].astype(jnp.float32)).astype(jnp.bfloat16)
    scaled_pad = jnp.concatenate([scaled.reshape(slot_count, model_width), jnp.zeros((1, model_width), scaled.dtype)], axis=0)
    inverse = jnp.zeros((model_width,), jnp.int32).at[new_place].set(jnp.arange(model_width, dtype=jnp.int32))

    def one_expert(total, expert):
        positions = jnp.nonzero(flat_ids == expert, size=most_rows, fill_value=slot_count)[0].astype(jnp.int32)
        picked = jnp.take(acts_pad, positions, axis=0)
        weight = jnp.take(weight_old[expert], old_place, axis=0)
        result = jnp.dot(picked, weight.T, preferred_element_type=jnp.float32).astype(jnp.bfloat16)
        weighted = jnp.take(flat_gates, positions)[:, None] * result.astype(jnp.float32)
        total = total.at[positions // top_count].add(weighted, mode='drop')
        gradient = jnp.dot(jnp.take(scaled_pad, positions, axis=0).T, picked, preferred_element_type=jnp.float32)
        new_weight, new_one, new_two = adamw_step(weight, jnp.take(first_old[expert], old_place, axis=0), jnp.take(second_old[expert], old_place, axis=0), gradient)
        return (total, (jnp.take(new_weight, inverse, axis=0), jnp.take(new_one, inverse, axis=0), jnp.take(new_two, inverse, axis=0)))
    total, stacked = lax.scan(one_expert, jnp.zeros((tokens, model_width), jnp.float32), jnp.arange(EXPERTS, dtype=jnp.int32))
    return (total.astype(jnp.bfloat16), stacked[0], stacked[1], stacked[2])
```

```python
import jax
import jax.numpy as jnp
from jax import lax
from jax.experimental import pallas as pl
from jax.experimental.pallas import tpu as pltpu
from jax.sharding import PartitionSpec as P

beta_one = 0.9
beta_two = 0.95
adam_eps = 1e-08
learn_rate = 0.001
weight_decay = 0.1
bias_one = 1.0 - 0.9**50 * 0.9**50
bias_two = 1.0 - 0.95**50 * 0.95**50

RING = 4
NEAR = [[far * RING + near for near in range(RING)] for far in range(RING)]
FAR = [[far * RING + near for far in range(RING)] for near in range(RING)]

VMEM_BYTES = 48 * 1024 * 1024
CONTRACT_LAST = (((1,), (1,)), ((), ()))
CONTRACT_FIRST = (((0,), (0,)), ((), ()))


def dot(left, right, dims=(((1,), (0,)), ((), ()))):
    return lax.dot_general(left, right, dims, preferred_element_type=jnp.float32)


def whole():
    return pl.BlockSpec(memory_space=pltpu.VMEM)


def gather_dp(piece):
    far = lax.all_gather(piece, "dp", axis=0, axis_index_groups=FAR)
    return lax.all_gather(far, "dp", axis=0, axis_index_groups=NEAR)


def forward_kernel(acts_ref, weight_ref, rows_ref, out_ref):
    near, far, rows, lanes = acts_ref.shape
    half = lanes // 2
    source = lax.broadcasted_iota(jnp.int32, (2 * lanes, lanes), 0)
    target = lax.broadcasted_iota(jnp.int32, (2 * lanes, lanes), 1)
    picked = jnp.where(target < half, target, target + half)
    shuffles = [(source == picked + side * half).astype(jnp.bfloat16) for side in range(2)]
    for z in range(far):
        for x in range(0, near, 2):
            pair = jnp.concatenate([acts_ref[x, z], acts_ref[x + 1, z]], axis=1)
            first = (z * near + x) * half
            for side in range(2):
                rows_ref[side, :, first : first + lanes] = dot(pair, shuffles[side]).astype(
                    jnp.bfloat16
                )
    for side in range(2):
        result = dot(rows_ref[side], weight_ref[...], CONTRACT_LAST).astype(jnp.bfloat16)
        blocks, slots, width = out_ref.shape
        out_ref[:, side * (slots // 2) : (side + 1) * (slots // 2), :] = result.reshape(
            blocks, slots // 2, width
        )


def update_kernel(rows_ref, scaled_ref, weight_ref, moments_ref, place_ref, w_ref, m_ref, v_ref):
    blocks, slots, width = scaled_ref.shape
    half = slots // 2
    unpack = place_ref[...]
    lanes = 256
    for first in range(0, w_ref.shape[1], lanes):
        piece = slice(first, first + lanes)
        gradient = jnp.zeros((width, lanes), jnp.float32)
        for side in range(2):
            scaled = scaled_ref[:, side * half : (side + 1) * half, :].reshape(blocks * half, width)
            gradient += dot(scaled, rows_ref[side, :, piece], CONTRACT_FIRST)
        weight = weight_ref[:, piece].astype(jnp.float32)
        one = dot(unpack, moments_ref[0, :, piece])
        two = dot(unpack, moments_ref[1, :, piece])
        one_next = beta_one * one + (1.0 - beta_one) * gradient
        two_next = beta_two * two + (1.0 - beta_two) * gradient * gradient
        update = (
            one_next / bias_one / (jnp.sqrt(two_next / bias_two) + adam_eps)
            + weight_decay * weight
        )
        w_ref[:, piece] = (weight - learn_rate * update).astype(jnp.bfloat16)
        m_ref[:, piece] = one_next.astype(jnp.bfloat16)
        v_ref[:, piece] = two_next.astype(jnp.bfloat16)


def shards(
    hidden_acts,
    expert_ids,
    gate_weights,
    cotangent,
    weight_old,
    first_old,
    second_old,
    old_place,
    new_place,
):
    n_expert = lax.axis_size("expert")
    n_data = lax.axis_size("dp")
    me = lax.axis_index("dp")
    tok_rows, top_count, piece_width = hidden_acts.shape
    hidden = weight_old.shape[2]
    width = cotangent.shape[1]
    model_width = width * n_data
    old_group = 3 * n_data // 4
    move_cap = (width + old_group - 1) // old_group
    old_rows = weight_old.shape[1]
    slot_count = tok_rows * top_count
    cap = 2 * slot_count // n_expert
    bf16 = jnp.bfloat16

    def count(size):
        return jnp.arange(size, dtype=jnp.int32)

    ids = expert_ids.reshape(slot_count)
    earlier = (ids[:, None] == ids[None, :]) & (count(slot_count)[None, :] < count(slot_count)[:, None])
    slot_of = ids * cap + jnp.sum(earlier.astype(jnp.int32), axis=1)
    row = count(n_expert * cap // 2)
    low = row // (cap // 2) * cap + row % (cap // 2)
    acts_flat = hidden_acts.reshape(slot_count, piece_width)
    sides = [
        dot((low[:, None] + side * (cap // 2) == slot_of[None, :]).astype(bf16), acts_flat).astype(bf16)
        for side in range(2)
    ]
    packed = jnp.concatenate(sides, axis=1).reshape(n_expert, cap // 2, 2 * piece_width)
    arrived = lax.all_to_all(packed, "expert", split_axis=0, concat_axis=0, tiled=True)

    moved = old_place[None, :] == me * old_rows + count(old_rows)[:, None]
    new_of_old = jnp.sum(jnp.where(moved, new_place[None, :] + 1, 0), axis=1) - 1
    target = jnp.where(new_of_old >= 0, new_of_old // width, n_data)
    before = (target[:, None] == target[None, :]) & (count(old_rows)[None, :] < count(old_rows)[:, None])
    send_slot = jnp.where(
        target < n_data, target * move_cap + jnp.sum(before.astype(jnp.int32), axis=1), -1
    )
    pack = (count(n_data * move_cap)[:, None] == send_slot[None, :]).astype(bf16)

    held = new_place[None, :] == me * width + count(width)[:, None]
    model_row = jnp.sum(jnp.where(held, count(model_width)[None, :], 0), axis=1)
    origin = jnp.sum(jnp.where(held, old_place[None, :], 0), axis=1)
    owner = origin // old_rows
    lower = (owner[:, None] == owner[None, :]) & (origin[None, :] < origin[:, None])
    recv_slot = owner * move_cap + jnp.sum(lower.astype(jnp.int32), axis=1)
    unpack = (recv_slot[:, None] == count(n_data * move_cap)[None, :]).astype(bf16)

    def pack_state(source):
        return dot(pack, source[0]).astype(bf16).reshape(n_data, move_cap, hidden)

    weight_got = lax.all_to_all(
        pack_state(weight_old), "dp", split_axis=0, concat_axis=0, tiled=True
    ).reshape(n_data * move_cap, hidden)
    moments = jnp.concatenate([pack_state(first_old), pack_state(second_old)], axis=1)
    moments_got = lax.all_to_all(moments, "dp", split_axis=0, concat_axis=0, tiled=True)
    moments_got = (
        moments_got.reshape(n_data, 2, move_cap, hidden)
        .transpose(1, 0, 2, 3)
        .reshape(2, n_data * move_cap, hidden)
    )

    ring = n_data // RING
    block = (count(ring)[None, :] * RING + count(RING)[:, None]).reshape(n_data)
    column = block[:, None] * width + count(width)[None, :]

    def pick(blocks, wanted):
        hot = (column[:, :, None] == wanted[None, None, :]).astype(bf16)
        return jnp.einsum(
            "jtc,jcn->tn",
            blocks.reshape(n_data, tok_rows, width),
            hot,
            preferred_element_type=jnp.float32,
        )

    chosen = pick(gather_dp(cotangent), model_row).astype(bf16)
    gates = gate_weights.reshape(slot_count)
    places = count(n_expert * cap)[:, None] == slot_of[None, :]
    gate_packed = jnp.sum(jnp.where(places, gates[None, :], 0.0), axis=1)
    token_of = jnp.max(
        jnp.where(
            count(n_expert * cap)[:, None, None] == slot_of.reshape(tok_rows, top_count).T[None], 1, 0
        ),
        axis=1,
    ).astype(bf16)
    scaled = (gate_packed[:, None] * dot(token_of, chosen)).astype(bf16)
    scaled_got = lax.all_to_all(
        scaled.reshape(n_expert, cap, width), "expert", split_axis=0, concat_axis=0, tiled=True
    )

    weight_now = dot(unpack, weight_got).astype(bf16)
    acts_all = gather_dp(arrived.reshape(n_expert * cap // 2, 2 * piece_width))
    rows, outputs = pl.pallas_call(
        forward_kernel,
        out_shape=(
            jax.ShapeDtypeStruct((2, n_expert * cap // 2, hidden), bf16),
            jax.ShapeDtypeStruct((n_expert, cap, width), bf16),
        ),
        in_specs=[whole()] * 2,
        out_specs=(whole(), whole()),
        compiler_params=pltpu.CompilerParams(vmem_limit_bytes=VMEM_BYTES),
        cost_estimate=pl.CostEstimate(
            flops=2 * n_expert * cap * hidden * (width + 512),
            bytes_accessed=5 * 1024 * 1024,
            transcendentals=0,
        ),
        name="forward",
    )(acts_all, weight_now)
    returned = lax.all_to_all(outputs, "expert", split_axis=0, concat_axis=0, tiled=True)
    mine = (slot_of[:, None] == count(n_expert * cap)[None, :]).astype(bf16)
    per_slot = dot(mine, returned.reshape(n_expert * cap, width)).reshape(tok_rows, top_count, width)
    combined_part = jnp.sum(gate_weights[:, :, None] * per_slot, axis=1).astype(bf16)
    place_block = lax.dynamic_slice_in_dim(new_place, me * width, width)
    combined = pick(gather_dp(combined_part), place_block).astype(bf16)

    state = jax.ShapeDtypeStruct((width, hidden), bf16)
    new_weight, new_one, new_two = pl.pallas_call(
        update_kernel,
        out_shape=(state, state, state),
        in_specs=[whole()] * 5,
        out_specs=(whole(), whole(), whole()),
        compiler_params=pltpu.CompilerParams(vmem_limit_bytes=VMEM_BYTES),
        cost_estimate=pl.CostEstimate(
            flops=2 * n_expert * cap * hidden * width,
            bytes_accessed=6 * 1024 * 1024,
            transcendentals=width * hidden,
        ),
        name="update",
    )(rows, scaled_got, weight_now, moments_got, unpack)
    return (combined, new_weight[None], new_one[None], new_two[None])


def solution(mesh):
    return jax.shard_map(
        shards,
        mesh=mesh,
        in_specs=(
            P("expert", None, "dp"),
            P("expert", None),
            P("expert", None),
            P("expert", "dp"),
            P("expert", "dp", None),
            P("expert", "dp", None),
            P("expert", "dp", None),
            P(),
            P(),
        ),
        out_specs=(
            P("expert", "dp"),
            P("expert", "dp", None),
            P("expert", "dp", None),
            P("expert", "dp", None),
        ),
        check_vma=False,
    )
```

```python
import jax
import jax.numpy as jnp
from jax import lax
from jax.experimental import pallas as pl
from jax.experimental.pallas import tpu as pltpu
from jax.sharding import PartitionSpec as P

beta_one = 0.9
beta_two = 0.95
adam_eps = 1e-08
learn_rate = 0.001
weight_decay = 0.1
bias_one = 1.0 - 0.9**50 * 0.9**50
bias_two = 1.0 - 0.95**50 * 0.95**50

RING = 4
NEAR = [[far * RING + near for near in range(RING)] for far in range(RING)]
FAR = [[far * RING + near for far in range(RING)] for near in range(RING)]

LANES = 128
CHUNKS = 8
ROWS = 16

VMEM_BYTES = 48 * 1024 * 1024
CONTRACT_LAST = (((1,), (1,)), ((), ()))
CONTRACT_FIRST = (((0,), (0,)), ((), ()))


def dot(left, right, dims=(((1,), (0,)), ((), ()))):
    return lax.dot_general(left, right, dims, preferred_element_type=jnp.float32)


def whole():
    return pl.BlockSpec(memory_space=pltpu.VMEM)


def gather_far(piece):
    return lax.all_gather(piece, "dp", axis=0, axis_index_groups=FAR)


def gather_near(piece):
    return lax.all_gather(piece, "dp", axis=0, axis_index_groups=NEAR)


def gather_whole(piece):
    every = lax.all_gather(piece, "dp", axis=0)
    return every.reshape(RING, RING, *piece.shape).swapaxes(0, 1)


def send_far(piece, step):
    pairs = [
        (far * RING + near, (far + step) % RING * RING + near)
        for far in range(RING)
        for near in range(RING)
    ]
    return lax.ppermute(piece, "dp", pairs)


def iota(shape, axis):
    return lax.broadcasted_iota(jnp.int32, shape, axis)


def to_row(column):
    size = column.shape[0]
    same = iota((size, size), 0) == iota((size, size), 1)
    return jnp.sum(jnp.where(same, column, 0), axis=0, keepdims=True)


def pick(blocks_ref, wanted):
    near, far, width, tokens = blocks_ref.shape
    column = iota((wanted.shape[0], width), 1)
    total = jnp.zeros((wanted.shape[0], tokens), jnp.float32)
    for x in range(near):
        for z in range(far):
            hot = (column + (z * near + x) * width == wanted).astype(jnp.bfloat16)
            total += dot(hot, blocks_ref[x, z])
    return total


def slot_hot(slot_ref, slots):
    top, tokens = slot_ref.shape
    here = iota((slots, tokens), 0)
    return jnp.concatenate(
        [(here == slot_ref[k : k + 1, :]).astype(jnp.bfloat16) for k in range(top)], axis=1
    )


def dispatch_kernel(acts_ref, ids_ref, packed_ref, slot_ref):
    experts, half, wide = packed_ref.shape
    top, tokens = ids_ref.shape
    piece, cap = wide // 2, 2 * half
    every = top * tokens
    choices = jnp.concatenate([ids_ref[k : k + 1, :] for k in range(top)], axis=1)
    named = iota((experts, every), 0) == choices
    ahead = (iota((every, every), 0) < iota((every, every), 1)).astype(jnp.bfloat16)
    rank = dot(named.astype(jnp.bfloat16), ahead)
    rank = jnp.sum(jnp.where(named, rank, 0.0), axis=0, keepdims=True).astype(jnp.int32)
    slot = choices * cap + rank
    for k in range(top):
        slot_ref[k : k + 1, :] = slot[:, k * tokens : (k + 1) * tokens]
    features = jnp.concatenate(
        [acts_ref[k * piece : (k + 1) * piece, :] for k in range(top)], axis=1
    )
    row = iota((experts * half, every), 0)
    row = row // half * cap + row % half
    sides = [
        dot((row + side * half == slot).astype(jnp.bfloat16), features, CONTRACT_LAST)
        for side in range(2)
    ]
    packed = jnp.concatenate(sides, axis=1).astype(jnp.bfloat16)
    packed_ref[...] = packed.reshape(packed_ref.shape)


def scale_kernel(blocks_ref, wanted_ref, gates_ref, slot_ref, packed_ref):
    experts, cap, width = packed_ref.shape
    top = gates_ref.shape[0]
    chosen = pick(blocks_ref, wanted_ref[...])
    scaled = jnp.concatenate(
        [(gates_ref[k : k + 1, :] * chosen).astype(jnp.bfloat16) for k in range(top)], axis=1
    )
    hot = slot_hot(slot_ref, experts * cap)
    packed_ref[...] = dot(hot, scaled, CONTRACT_LAST).astype(jnp.bfloat16).reshape(packed_ref.shape)


def tables(me, old_ref, new_ref, old_rows, width, cap):
    blocks, lanes = old_ref.shape
    far = me // RING
    leaving = jnp.zeros((old_rows, lanes), jnp.int32)
    origin = jnp.zeros((width, lanes), jnp.int32)
    model = jnp.zeros((width, lanes), jnp.int32)
    own = jnp.zeros((width, lanes), jnp.int32)
    for i in range(blocks):
        old, new = old_ref[i : i + 1, :], new_ref[i : i + 1, :]
        number = iota((1, lanes), 1) + i * lanes
        leaving += jnp.where(old - me * old_rows == iota((old_rows, lanes), 0), new + 1, 0)
        row = iota((width, lanes), 0)
        held = new - me * width == row
        origin += jnp.where(held, old, 0)
        model += jnp.where(held, number, 0)
        own += jnp.where(number - me * width == row, new, 0)
    leaving, origin, model, own = [
        jnp.sum(part, axis=1, keepdims=True) for part in (leaving, origin, model, own)
    ]
    leaving_row = to_row(leaving)
    target, target_row = (leaving - 1) // width, (leaving_row - 1) // width
    size = (old_rows, old_rows)
    rank = jnp.sum(
        ((target == target_row) & (iota(size, 0) < iota(size, 1)) & (leaving > 0)).astype(jnp.int32),
        axis=0,
        keepdims=True,
    )
    step = (target_row // RING - far + RING) % RING
    first = target_row % RING * RING
    send = jnp.where(leaving_row > 0, (first + target_row // RING) * cap + rank, -1)
    send_step = jnp.where(leaving_row > 0, (first + step) * cap + rank, -1)
    origin_row = to_row(origin)
    owner, owner_row = origin // old_rows, origin_row // old_rows
    rank = jnp.sum(
        ((owner == owner_row) & (origin_row < origin)).astype(jnp.int32), axis=1, keepdims=True
    )
    step = (far - owner // RING + RING) % RING
    recv = owner * cap + rank
    recv_step = (step * RING + owner % RING) * cap + rank
    return send, send_step, recv, recv_step, model, own


def pack_lines(source, slot, devices, cap):
    count = source.shape[0]
    rest = cap - ROWS
    lines = rest * CHUNKS
    index = iota((devices * ROWS, count), 0)
    hot = (index // ROWS * cap + index % ROWS == slot).astype(jnp.bfloat16)
    main = dot(hot, source)
    index = iota((devices * lines, count), 0)
    hot = (index // lines * cap + ROWS + index % rest == slot).astype(jnp.bfloat16)
    tail_rows = dot(hot, source)
    line = iota((devices * lines, LANES), 0) % lines // rest
    tail = jnp.zeros((devices * lines, LANES), jnp.float32)
    for c in range(CHUNKS):
        tail = jnp.where(line == c, tail_rows[:, c * LANES : (c + 1) * LANES], tail)
    mains = [main[:, c * LANES : (c + 1) * LANES].reshape(devices, ROWS, LANES) for c in range(CHUNKS)]
    return mains, tail.reshape(devices, lines, LANES)


def pack_kernel(me_ref, old_ref, new_ref, *refs):
    sources, (out_ref, recv_ref, recv_step_ref, model_ref, own_ref, held, sems) = refs[:3], refs[3:]
    copies = [pltpu.make_async_copy(source, held.at[i], sems.at[i]) for i, source in enumerate(sources)]
    for copy in copies:
        copy.start()
    devices, lines, _ = out_ref.shape
    cap = lines // (CHUNKS * len(sources))
    send, send_step, recv_ref[...], recv_step_ref[...], model_ref[...], own_ref[...] = tables(
        me_ref[0], old_ref, new_ref, held.shape[1], recv_ref.shape[0], cap
    )
    for copy in copies:
        copy.wait()
    place, tails = 0, []
    for number in range(len(sources)):
        mains, tail = pack_lines(held[number], send_step if number else send, devices, cap)
        for main in mains:
            out_ref[:, place : place + ROWS, :] = main.astype(jnp.bfloat16)
            place += ROWS
        tails.append(tail)
    out_ref[:, place:, :] = jnp.concatenate(tails, axis=1).astype(jnp.bfloat16)


class Arrived:
    def __init__(self, refs, recv, count):
        devices = sum(ref.shape[0] for ref in refs)
        lines = refs[0].shape[1]
        cap = lines // (CHUNKS * count)
        self.refs = refs
        width = recv.shape[0]
        rest = cap - ROWS
        self.lines = rest * CHUNKS
        index = iota((width, devices * ROWS), 1)
        self.main = (index // ROWS * cap + index % ROWS == recv).astype(jnp.bfloat16)
        index = iota((width, devices * self.lines), 1)
        self.tail = (index // self.lines * cap + ROWS + index % rest == recv).astype(jnp.bfloat16)
        self.chunk = iota((devices * self.lines, LANES), 0) % self.lines // rest
        start = count * CHUNKS * ROWS
        self.rest = jnp.concatenate([ref[:, start:, :].astype(jnp.float32) for ref in refs], axis=0)

    def piece(self, number, c):
        first = (number * CHUNKS + c) * ROWS
        rows = [ref[:, first : first + ROWS, :].reshape(-1, LANES) for ref in self.refs]
        rest = self.rest[:, number * self.lines : (number + 1) * self.lines, :].reshape(-1, LANES)
        rest = jnp.where(self.chunk == c, rest, 0.0).astype(jnp.bfloat16)
        return dot(self.main, jnp.concatenate(rows, axis=0)) + dot(self.tail, rest)


def unpack_kernel(got_ref, recv_ref, weight_ref):
    arrived = Arrived([got_ref], recv_ref[...], 1)
    for c in range(CHUNKS):
        weight_ref[:, c * LANES : (c + 1) * LANES] = arrived.piece(0, c).astype(jnp.bfloat16)


def forward_kernel(acts_ref, weight_ref, rows_ref, out_ref):
    near, far, rows, lanes = acts_ref.shape
    half = lanes // 2
    source, target = iota((2 * lanes, lanes), 0), iota((2 * lanes, lanes), 1)
    picked = jnp.where(target < half, target, target + half)
    shuffles = [(source == picked + side * half).astype(jnp.bfloat16) for side in range(2)]
    for z in range(far):
        for x in range(0, near, 2):
            pair = jnp.concatenate([acts_ref[x, z], acts_ref[x + 1, z]], axis=1)
            first = (z * near + x) * half
            for side in range(2):
                rows_ref[side, :, first : first + lanes] = dot(pair, shuffles[side]).astype(
                    jnp.bfloat16
                )
    blocks, slots, width = out_ref.shape
    for side in range(2):
        result = dot(rows_ref[side], weight_ref[...], CONTRACT_LAST).astype(jnp.bfloat16)
        out_ref[:, side * (slots // 2) : (side + 1) * (slots // 2), :] = result.reshape(
            blocks, slots // 2, width
        )


def combine_kernel(returned_ref, gates_ref, slot_ref, out_ref):
    experts, cap, width = returned_ref.shape
    top, tokens = gates_ref.shape
    rows = returned_ref[...].reshape(experts * cap, width)
    each = dot(rows, slot_hot(slot_ref, experts * cap), CONTRACT_FIRST)
    total = jnp.zeros((width, tokens), jnp.float32)
    for k in range(top):
        total += gates_ref[k : k + 1, :] * each[:, k * tokens : (k + 1) * tokens]
    out_ref[...] = total.astype(jnp.bfloat16)


def pick_kernel(blocks_ref, wanted_ref, out_ref):
    out_ref[...] = pick(blocks_ref, wanted_ref[...]).astype(jnp.bfloat16)


def gradient_kernel(rows_ref, scaled_ref, out_ref):
    blocks, slots, width = scaled_ref.shape
    half = slots // 2
    total = jnp.zeros(out_ref.shape, jnp.float32)
    for side in range(2):
        scaled = scaled_ref[:, side * half : (side + 1) * half, :].reshape(blocks * half, width)
        total += dot(scaled, rows_ref[side], CONTRACT_FIRST)
    out_ref[...] = total


def update_kernel(gradient_ref, weight_ref, *refs):
    recv_ref, w_ref, m_ref, v_ref = refs[RING:]
    arrived = Arrived(refs[:RING], recv_ref[...], 2)
    for c in range(CHUNKS):
        piece = slice(c * LANES, (c + 1) * LANES)
        gradient = gradient_ref[:, piece]
        weight = weight_ref[:, piece].astype(jnp.float32)
        one_next = beta_one * arrived.piece(0, c) + (1.0 - beta_one) * gradient
        two_next = beta_two * arrived.piece(1, c) + (1.0 - beta_two) * gradient * gradient
        update = (
            one_next / bias_one / (jnp.sqrt(two_next / bias_two) + adam_eps)
            + weight_decay * weight
        )
        w_ref[:, piece] = (weight - learn_rate * update).astype(jnp.bfloat16)
        m_ref[:, piece] = one_next.astype(jnp.bfloat16)
        v_ref[:, piece] = two_next.astype(jnp.bfloat16)


def call(kernel, name, out_shape, *args, flops=0, scalars=0, apart=(), scratch=(), order=()):
    several = isinstance(out_shape, tuple)
    count = len(args)

    def body(*refs):
        kernel(*refs[:count], *refs[count + len(order) :])

    specs = [pl.BlockSpec(memory_space=pltpu.SMEM)] * scalars + [whole()] * (count - scalars)
    for i in apart:
        specs[i] = pl.BlockSpec(memory_space=pltpu.HBM)
    return pl.pallas_call(
        body,
        out_shape=out_shape,
        in_specs=specs + [pl.BlockSpec(memory_space=pl.ANY)] * len(order),
        out_specs=tuple(whole() for _ in out_shape) if several else whole(),
        scratch_shapes=scratch,
        compiler_params=pltpu.CompilerParams(vmem_limit_bytes=VMEM_BYTES),
        cost_estimate=pl.CostEstimate(flops=flops, bytes_accessed=1024, transcendentals=0),
        name=name,
    )(*args, *order)


def shards(
    hidden_acts,
    expert_ids,
    gate_weights,
    cotangent,
    weight_old,
    first_old,
    second_old,
    old_place,
    new_place,
):
    n_expert = lax.axis_size("expert")
    n_data = lax.axis_size("dp")
    me = lax.axis_index("dp")
    tok_rows, top_count, piece = hidden_acts.shape
    hidden = weight_old.shape[2]
    width = cotangent.shape[1]
    old_group = 3 * n_data // 4
    move_cap = (width + old_group - 1) // old_group
    cap = 2 * tok_rows * top_count // n_expert
    slots = n_expert * cap
    int32 = jnp.int32

    def shape(*sizes, dtype=jnp.bfloat16):
        return jax.ShapeDtypeStruct(sizes, dtype)

    def exchange(array, axis, groups=None):
        return lax.all_to_all(
            array, axis, split_axis=0, concat_axis=0, tiled=True, axis_index_groups=groups
        )

    rows = slots // 2
    packed, slot = call(
        dispatch_kernel,
        "dispatch",
        (shape(n_expert, cap // 2, 2 * piece), shape(top_count, tok_rows, dtype=int32)),
        hidden_acts.transpose(1, 2, 0).reshape(top_count * piece, tok_rows),
        expert_ids.T,
    )
    arrived = exchange(packed, "expert")

    lines = hidden // LANES * move_cap
    old_rows = weight_old.shape[1]
    column = shape(width, 1, dtype=int32)
    sent, recv, recv_step, model, own = call(
        pack_kernel,
        "pack",
        (shape(n_data, 3 * lines, LANES), column, column, column, column),
        me[None].astype(int32),
        old_place.reshape(-1, LANES),
        new_place.reshape(-1, LANES),
        weight_old[0],
        first_old[0],
        second_old[0],
        scalars=1,
        apart=(3, 4, 5),
        scratch=[pltpu.VMEM((3, old_rows, hidden), jnp.bfloat16), pltpu.SemaphoreType.DMA((3,))],
    )
    sent, arrived = lax.optimization_barrier((sent, arrived))
    state = exchange(sent.reshape(RING, RING, 3 * lines, LANES), "dp", NEAR)

    both = jnp.concatenate([arrived.reshape(rows, 2 * piece), cotangent.T], axis=0)
    both_far, state = lax.optimization_barrier((gather_far(both), state))
    acts_all = gather_near(both_far[:, :rows])
    cot_far = both_far[:, rows:]
    gates = gate_weights.T

    block = ROWS * CHUNKS
    rest = lines - block
    weight_sent = jnp.concatenate(
        [state[:, :, :block], state[:, :, 3 * block : 3 * block + rest]], axis=2
    ).transpose(1, 0, 2, 3)
    weight_got = exchange(weight_sent, "dp", FAR).reshape(n_data, lines, LANES)
    weight_now = call(unpack_kernel, "unpack", shape(width, hidden), weight_got, recv)
    moments_got = []
    for step in range(RING):
        moments = jnp.concatenate(
            [state[:, step, block : 3 * block], state[:, step, 3 * block + rest :]], axis=1
        )
        moments_got.append(send_far(moments, step) if step else moments)

    def tail(gather):
        def run(acts_all, weight_now, cot_far, slot, gates, model, own):
            rows_now, outputs = call(
                forward_kernel,
                "forward",
                (shape(2, rows, hidden), shape(n_expert, cap, width)),
                acts_all,
                weight_now,
            )
            returned = exchange(outputs, "expert")
            scaled = call(
                scale_kernel,
                "scale",
                shape(n_expert, cap, width),
                gather_near(cot_far),
                model,
                gates,
                slot,
            )
            scaled, returned = lax.optimization_barrier((scaled, returned))
            scaled_got = exchange(scaled, "expert")
            part = call(combine_kernel, "combine", shape(width, tok_rows), returned, gates, slot)
            gradient = call(
                gradient_kernel,
                "gradient",
                shape(width, hidden, dtype=jnp.float32),
                rows_now,
                scaled_got,
            )
            combined = call(pick_kernel, "pick", shape(width, tok_rows), gather(part), own)
            return combined, gradient

        return run

    combined, gradient = lax.cond(
        new_place[0] >= 0,
        tail(lambda part: gather_near(gather_far(part))),
        tail(gather_whole),
        acts_all,
        weight_now,
        cot_far,
        slot,
        gates,
        model,
        own,
    )
    combined = combined.T
    new_weight, new_one, new_two = call(
        update_kernel,
        "update",
        (shape(width, hidden),) * 3,
        gradient,
        weight_now,
        *moments_got,
        recv_step,
    )
    return (combined, new_weight[None], new_one[None], new_two[None])


def solution(mesh):
    return jax.shard_map(
        shards,
        mesh=mesh,
        in_specs=(
            P("expert", None, "dp"),
            P("expert", None),
            P("expert", None),
            P("expert", "dp"),
            P("expert", "dp", None),
            P("expert", "dp", None),
            P("expert", "dp", None),
            P(),
            P(),
        ),
        out_specs=(
            P("expert", "dp"),
            P("expert", "dp", None),
            P("expert", "dp", None),
            P("expert", "dp", None),
        ),
        check_vma=False,
    )
```

```python
import jax
import jax.numpy as jnp
from jax import lax
from jax.experimental import pallas as pl
from jax.experimental.pallas import tpu as pltpu
from jax.sharding import PartitionSpec as P

beta_one = 0.9
beta_two = 0.95
adam_eps = 1e-08
learn_rate = 0.001
weight_decay = 0.1
bias_one = 1.0 - 0.9**50 * 0.9**50
bias_two = 1.0 - 0.95**50 * 0.95**50

RING = 4
OLD_FAR = 3 * RING // 4
NEAR = [[far * RING + near for near in range(RING)] for far in range(RING)]
FAR = [[far * RING + near for far in range(RING)] for near in range(RING)]

LANES = 128
CHUNKS = 8
ROWS = 16

VMEM_BYTES = 48 * 1024 * 1024
PACK_VMEM_BYTES = 60 * 1024 * 1024
CONTRACT_LAST = (((1,), (1,)), ((), ()))
CONTRACT_FIRST = (((0,), (0,)), ((), ()))


def dot(left, right, dims=(((1,), (0,)), ((), ()))):
    return lax.dot_general(left, right, dims, preferred_element_type=jnp.float32)


def whole():
    return pl.BlockSpec(memory_space=pltpu.VMEM)


def gather_far(piece):
    return lax.all_gather(piece, "dp", axis=0, axis_index_groups=FAR)


def gather_near(piece):
    return lax.all_gather(piece, "dp", axis=0, axis_index_groups=NEAR)


def send_far(piece, step):
    pairs = [
        (far * RING + near, (far + step) % RING * RING + near)
        for far in range(OLD_FAR)
        for near in range(RING)
    ]
    return lax.ppermute(piece, "dp", pairs)


def iota(shape, axis):
    return lax.broadcasted_iota(jnp.int32, shape, axis)


def to_row(column):
    size = column.shape[0]
    same = iota((size, size), 0) == iota((size, size), 1)
    return jnp.sum(jnp.where(same, column, 0), axis=0, keepdims=True)


def pick(blocks_ref, wanted, first=0):
    near, far, every, tokens = blocks_ref.shape
    width = every - first
    column = iota((wanted.shape[0], width), 1)
    total = jnp.zeros((wanted.shape[0], tokens), jnp.float32)
    for x in range(near):
        for z in range(far):
            hot = (column + (z * near + x) * width == wanted).astype(jnp.bfloat16)
            total += dot(hot, blocks_ref[x, z, first:, :])
    return total


def slot_hot(slot_ref, slots):
    top, tokens = slot_ref.shape
    here = iota((slots, tokens), 0)
    return jnp.concatenate(
        [(here == slot_ref[k : k + 1, :]).astype(jnp.bfloat16) for k in range(top)], axis=1
    )


def dispatch_kernel(acts_ref, ids_ref, packed_ref, slot_ref):
    experts, half, wide = packed_ref.shape
    top, tokens = ids_ref.shape
    piece, cap = wide // 2, 2 * half
    every = top * tokens
    choices = jnp.concatenate([ids_ref[k : k + 1, :] for k in range(top)], axis=1)
    named = iota((experts, every), 0) == choices
    ahead = (iota((every, every), 0) < iota((every, every), 1)).astype(jnp.bfloat16)
    rank = dot(named.astype(jnp.bfloat16), ahead)
    rank = jnp.sum(jnp.where(named, rank, 0.0), axis=0, keepdims=True).astype(jnp.int32)
    slot = choices * cap + rank
    for k in range(top):
        slot_ref[k : k + 1, :] = slot[:, k * tokens : (k + 1) * tokens]
    features = jnp.concatenate(
        [acts_ref[k * piece : (k + 1) * piece, :] for k in range(top)], axis=1
    )
    row = iota((experts * half, every), 0)
    row = row // half * cap + row % half
    sides = [
        dot((row + side * half == slot).astype(jnp.bfloat16), features, CONTRACT_LAST)
        for side in range(2)
    ]
    packed = jnp.concatenate(sides, axis=1).astype(jnp.bfloat16)
    packed_ref[...] = packed.reshape(packed_ref.shape)


def scale_kernel(blocks_ref, wanted_ref, gates_ref, slot_ref, packed_ref):
    experts, lines, lanes = packed_ref.shape
    cap, width = lines // 2, wanted_ref.shape[0]
    top, tokens = gates_ref.shape
    chosen = pick(blocks_ref, wanted_ref[...], blocks_ref.shape[2] - width)
    scaled = jnp.concatenate(
        [(gates_ref[k : k + 1, :] * chosen).astype(jnp.bfloat16) for k in range(top)], axis=1
    )
    hot = slot_hot(slot_ref, experts * cap)
    short = 2 * lanes - width
    scaled = jnp.concatenate([scaled, jnp.zeros((short, top * tokens), jnp.bfloat16)], axis=0)
    packed = dot(hot, scaled, CONTRACT_LAST).astype(jnp.bfloat16)
    for c in range(2):
        packed_ref[:, c * cap : (c + 1) * cap, :] = packed[:, c * lanes : (c + 1) * lanes].reshape(
            experts, cap, lanes
        )


def tables(me, old_ref, new_ref, old_rows, width, cap):
    blocks, lanes = old_ref.shape
    far = me // RING
    leaving = jnp.zeros((old_rows, lanes), jnp.int32)
    origin = jnp.zeros((width, lanes), jnp.int32)
    model = jnp.zeros((width, lanes), jnp.int32)
    for i in range(blocks):
        old, new = old_ref[i : i + 1, :], new_ref[i : i + 1, :]
        number = iota((1, lanes), 1) + i * lanes
        leaving += jnp.where(old - me * old_rows == iota((old_rows, lanes), 0), new + 1, 0)
        row = iota((width, lanes), 0)
        held = new - me * width == row
        origin += jnp.where(held, old, 0)
        model += jnp.where(held, number, 0)
    leaving, origin, model = [
        jnp.sum(part, axis=1, keepdims=True) for part in (leaving, origin, model)
    ]
    mine = RING * width // lanes
    same = iota((lanes, lanes), 0) == iota((lanes, lanes), 1)
    own = jnp.concatenate(
        [
            jnp.sum(jnp.where(same, old_ref[pl.ds(far * mine + i, 1), :], 0), axis=1, keepdims=True)
            for i in range(mine)
        ],
        axis=0,
    )
    leaving_row = to_row(leaving)
    target, target_row = (leaving - 1) // width, (leaving_row - 1) // width
    size = (old_rows, old_rows)
    rank = jnp.sum(
        ((target == target_row) & (iota(size, 0) < iota(size, 1)) & (leaving > 0)).astype(jnp.int32),
        axis=0,
        keepdims=True,
    )
    step = (target_row // RING - far + RING) % RING
    send = (target_row % RING * RING + step) * cap + rank
    send = jnp.where(leaving_row > 0, send, -1)
    origin_row = to_row(origin)
    owner, owner_row = origin // old_rows, origin_row // old_rows
    rank = jnp.sum(
        ((owner == owner_row) & (origin_row < origin)).astype(jnp.int32), axis=1, keepdims=True
    )
    step = (far - owner // RING + RING) % RING
    recv = (step * RING + owner % RING) * cap + rank
    return send, recv, model, own


def pack_lines(source, slot, devices, cap):
    count = source.shape[0]
    rest = cap - ROWS
    lines = rest * CHUNKS
    index = iota((devices * ROWS, count), 0)
    hot = (index // ROWS * cap + index % ROWS == slot).astype(jnp.bfloat16)
    main = dot(hot, source)
    index = iota((devices * lines, count), 0)
    hot = (index // lines * cap + ROWS + index % rest == slot).astype(jnp.bfloat16)
    tail_rows = dot(hot, source)
    line = iota((devices * lines, LANES), 0) % lines // rest
    tail = jnp.zeros((devices * lines, LANES), jnp.float32)
    for c in range(CHUNKS):
        tail = jnp.where(line == c, tail_rows[:, c * LANES : (c + 1) * LANES], tail)
    mains = [main[:, c * LANES : (c + 1) * LANES].reshape(devices, ROWS, LANES) for c in range(CHUNKS)]
    return mains, tail.reshape(devices, lines, LANES)


def pack_kernel(me_ref, old_ref, new_ref, *refs):
    sources, (out_ref, recv_ref, model_ref, own_ref, held, sems) = refs[:3], refs[3:]
    copies = [pltpu.make_async_copy(source, held.at[i], sems.at[i]) for i, source in enumerate(sources)]
    for copy in copies:
        copy.start()
    devices, lines, _ = out_ref.shape
    cap = lines // (CHUNKS * len(sources))
    send, recv_ref[...], model_ref[...], own_ref[...] = tables(
        me_ref[0], old_ref, new_ref, held.shape[1], recv_ref.shape[0], cap
    )
    for copy in copies:
        copy.wait()
    place, tails = 0, []
    for number in range(len(sources)):
        mains, tail = pack_lines(held[number], send, devices, cap)
        for main in mains:
            out_ref[:, place : place + ROWS, :] = main.astype(jnp.bfloat16)
            place += ROWS
        tails.append(tail)
    out_ref[:, place:, :] = jnp.concatenate(tails, axis=1).astype(jnp.bfloat16)


class Arrived:
    def __init__(self, refs, recv, count):
        devices = sum(ref.shape[0] for ref in refs)
        lines = refs[0].shape[1]
        cap = lines // (CHUNKS * count)
        self.refs = refs
        width = recv.shape[0]
        rest = cap - ROWS
        self.lines = rest * CHUNKS
        index = iota((width, devices * ROWS), 1)
        self.main = (index // ROWS * cap + index % ROWS == recv).astype(jnp.bfloat16)
        index = iota((width, devices * self.lines), 1)
        self.tail = (index // self.lines * cap + ROWS + index % rest == recv).astype(jnp.bfloat16)
        self.chunk = iota((devices * self.lines, LANES), 0) % self.lines // rest
        start = count * CHUNKS * ROWS
        self.rest = jnp.concatenate([ref[:, start:, :].astype(jnp.float32) for ref in refs], axis=0)

    def piece(self, number, c):
        first = (number * CHUNKS + c) * ROWS
        rows = [ref[:, first : first + ROWS, :].reshape(-1, LANES) for ref in self.refs]
        rest = self.rest[:, number * self.lines : (number + 1) * self.lines, :].reshape(-1, LANES)
        rest = jnp.where(self.chunk == c, rest, 0.0).astype(jnp.bfloat16)
        return dot(self.main, jnp.concatenate(rows, axis=0)) + dot(self.tail, rest)


def forward_kernel(acts_ref, weight_ref, scaled_ref, rows_ref, out_ref):
    near, far, _, lanes = acts_ref.shape
    rows = rows_ref.shape[1]
    half = lanes // 2
    source, target = iota((2 * lanes, lanes), 0), iota((2 * lanes, lanes), 1)
    picked = jnp.where(target < half, target, target + half)
    shuffles = [(source == picked + side * half).astype(jnp.bfloat16) for side in range(2)]
    for z in range(far):
        for x in range(0, near, 2):
            pair = jnp.concatenate([acts_ref[x, z, :rows, :], acts_ref[x + 1, z, :rows, :]], axis=1)
            first = (z * near + x) * half
            for side in range(2):
                rows_ref[side, :, first : first + lanes] = dot(pair, shuffles[side]).astype(
                    jnp.bfloat16
                )
    blocks, lines, _ = scaled_ref.shape
    part = lines // 4
    out_ref[:, 5 * part :, :] = scaled_ref[...]
    columns, hidden = weight_ref.shape
    short = 5 * lanes // 2 - columns
    weight = jnp.concatenate([weight_ref[...], jnp.zeros((short, hidden), jnp.bfloat16)], axis=0)
    last = []
    for side in range(2):
        result = dot(rows_ref[side], weight, CONTRACT_LAST).astype(jnp.bfloat16)
        for c in range(2):
            first = (2 * c + side) * part
            out_ref[:, first : first + part, :] = result[:, c * lanes : (c + 1) * lanes].reshape(
                blocks, part, lanes
            )
        last.append(result[:, 2 * lanes :])
    out_ref[:, 4 * part : 5 * part, :] = jnp.concatenate(last, axis=1).reshape(blocks, part, lanes)


def combine_kernel(returned_ref, gates_ref, slot_ref, out_ref):
    experts, lines, lanes = returned_ref.shape
    part = lines // 9
    top, tokens = gates_ref.shape
    hot = slot_hot(slot_ref, experts * 2 * part).reshape(experts, 2 * part, top * tokens)
    each = [0.0, 0.0, 0.0]
    for side in range(2):
        mine = hot[:, side * part : (side + 1) * part, :].reshape(experts * part, top * tokens)
        for c in range(3):
            first = (2 * c + side) * part if c < 2 else 4 * part
            rows = returned_ref[:, first : first + part, :].reshape(experts * part, lanes)
            if c == 2:
                rows = rows[:, side * (lanes // 2) : (side + 1) * (lanes // 2)]
            each[c] += dot(rows, mine, CONTRACT_FIRST)
    first = 0
    for piece in each:
        total = jnp.zeros((piece.shape[0], tokens), jnp.float32)
        for k in range(top):
            total += gates_ref[k : k + 1, :] * piece[:, k * tokens : (k + 1) * tokens]
        count = min(piece.shape[0], out_ref.shape[0] - first)
        out_ref[first : first + count, :] = total[:count].astype(jnp.bfloat16)
        first += count


def spread_kernel(me_ref, blocks_ref, own_ref, out_ref):
    far, width, tokens = blocks_ref.shape
    far = OLD_FAR
    near = me_ref[0] % RING
    column = iota((own_ref.shape[0], far * width), 1)
    column = (column // width * RING + near) * width + column % width
    hot = (column == own_ref[...]).astype(jnp.bfloat16)
    rows = dot(hot, blocks_ref[:far].reshape(far * width, tokens))
    out_ref[...] = rows.astype(jnp.bfloat16).reshape(out_ref.shape)


def sum_kernel(parts_ref, out_ref):
    out_ref[...] = jnp.sum(parts_ref[...].astype(jnp.float32), axis=0).astype(jnp.bfloat16)


def gradient_kernel(rows_ref, returned_ref, out_ref):
    blocks, lines, lanes = returned_ref.shape
    part = lines // 9
    total = 0.0
    for side in range(2):
        scaled = [
            returned_ref[:, (5 + 2 * c + side) * part : (6 + 2 * c + side) * part, :].reshape(
                blocks * part, lanes
            )
            for c in range(2)
        ]
        total += dot(jnp.concatenate(scaled, axis=1), rows_ref[side], CONTRACT_FIRST)
    out_ref[...] = total[: out_ref.shape[0]]


def update_kernel(gradient_ref, *refs):
    recv_ref, w_ref, m_ref, v_ref = refs[RING:]
    arrived = Arrived(refs[:RING], recv_ref[...], 3)
    for c in range(CHUNKS):
        piece = slice(c * LANES, (c + 1) * LANES)
        gradient = gradient_ref[:, piece]
        weight = arrived.piece(0, c)
        one_next = beta_one * arrived.piece(1, c) + (1.0 - beta_one) * gradient
        two_next = beta_two * arrived.piece(2, c) + (1.0 - beta_two) * gradient * gradient
        update = (
            one_next / bias_one / (jnp.sqrt(two_next / bias_two) + adam_eps)
            + weight_decay * weight
        )
        w_ref[:, piece] = (weight - learn_rate * update).astype(jnp.bfloat16)
        m_ref[:, piece] = one_next.astype(jnp.bfloat16)
        v_ref[:, piece] = two_next.astype(jnp.bfloat16)


def call(kernel, name, out_shape, *args, flops=0, scalars=0, apart=(), scratch=(), order=(), vmem=VMEM_BYTES):
    several = isinstance(out_shape, tuple)
    count = len(args)

    def body(*refs):
        kernel(*refs[:count], *refs[count + len(order) :])

    specs = [pl.BlockSpec(memory_space=pltpu.SMEM)] * scalars + [whole()] * (count - scalars)
    for i in apart:
        specs[i] = pl.BlockSpec(memory_space=pltpu.HBM)
    return pl.pallas_call(
        body,
        out_shape=out_shape,
        in_specs=specs + [pl.BlockSpec(memory_space=pl.ANY)] * len(order),
        out_specs=tuple(whole() for _ in out_shape) if several else whole(),
        scratch_shapes=scratch,
        compiler_params=pltpu.CompilerParams(vmem_limit_bytes=vmem),
        cost_estimate=pl.CostEstimate(flops=flops, bytes_accessed=1024, transcendentals=0),
        name=name,
    )(*args, *order)


def shards(
    hidden_acts,
    expert_ids,
    gate_weights,
    cotangent,
    weight_old,
    first_old,
    second_old,
    old_place,
    new_place,
):
    n_expert = lax.axis_size("expert")
    n_data = lax.axis_size("dp")
    me = lax.axis_index("dp")
    tok_rows, top_count, piece = hidden_acts.shape
    hidden = weight_old.shape[2]
    width = cotangent.shape[1]
    old_group = 3 * n_data // 4
    move_cap = (width + old_group - 1) // old_group
    cap = 2 * tok_rows * top_count // n_expert
    slots = n_expert * cap
    int32 = jnp.int32

    def shape(*sizes, dtype=jnp.bfloat16):
        return jax.ShapeDtypeStruct(sizes, dtype)

    def exchange(array, axis, groups=None):
        return lax.all_to_all(
            array, axis, split_axis=0, concat_axis=0, tiled=True, axis_index_groups=groups
        )

    rows = slots // 2
    packed, slot = call(
        dispatch_kernel,
        "dispatch",
        (shape(n_expert, cap // 2, 2 * piece), shape(top_count, tok_rows, dtype=int32)),
        hidden_acts.transpose(1, 2, 0).reshape(top_count * piece, tok_rows),
        expert_ids.T,
    )
    arrived = exchange(packed, "expert")

    device = me[None].astype(int32)
    lines = hidden // LANES * move_cap
    old_rows = weight_old.shape[1]
    column = shape(width, 1, dtype=int32)
    sent, recv, model, own = call(
        pack_kernel,
        "pack",
        (
            shape(n_data, 3 * lines, LANES),
            column,
            column,
            shape(RING * width, 1, dtype=int32),
        ),
        device,
        old_place.reshape(-1, LANES),
        new_place.reshape(-1, LANES),
        weight_old[0],
        first_old[0],
        second_old[0],
        scalars=1,
        vmem=PACK_VMEM_BYTES,
        apart=(3, 4, 5),
        scratch=[pltpu.VMEM((3, old_rows, hidden), jnp.bfloat16), pltpu.SemaphoreType.DMA((3,))],
    )
    sent, arrived = lax.optimization_barrier((sent, arrived))
    state = exchange(sent.reshape(RING, RING, 3 * lines, LANES), "dp", NEAR)

    both = jnp.concatenate([arrived.reshape(rows, 2 * piece), cotangent.T], axis=0)
    both_far, state = lax.optimization_barrier((gather_far(both), state))
    both_all = gather_near(both_far)
    gates = gate_weights.T

    scaled = call(
        scale_kernel, "scale", shape(n_expert, 2 * cap, LANES), both_all, model, gates, slot
    )

    state_got = [send_far(state[:, step], step) if step else state[:, 0] for step in range(RING)]

    def tail(forward_name):
        def run(both_all, weight, scaled, slot, gates):
            rows_now, outputs = call(
                forward_kernel,
                forward_name,
                (shape(2, rows, hidden), shape(n_expert, 9 * cap // 2, LANES)),
                both_all,
                weight,
                scaled,
            )
            returned = exchange(outputs, "expert")
            part = call(combine_kernel, "combine", shape(old_rows, tok_rows), returned, gates, slot)
            return rows_now, part, returned

        return run

    rows_now, part, returned = lax.cond(
        new_place[0] >= 0,
        tail("forward"),
        tail("forward_too"),
        both_all,
        weight_old[0],
        scaled,
        slot,
        gates,
    )
    part, state_got = lax.optimization_barrier((part, state_got))
    spread = call(
        spread_kernel,
        "spread",
        shape(RING, width, tok_rows),
        device,
        gather_far(part),
        own,
        scalars=1,
    )
    combined = call(sum_kernel, "sum", shape(width, tok_rows), exchange(spread, "dp", NEAR)).T
    gradient = call(
        gradient_kernel, "gradient", shape(width, hidden, dtype=jnp.float32), rows_now, returned
    )
    new_weight, new_one, new_two = call(
        update_kernel,
        "update",
        (shape(width, hidden),) * 3,
        gradient,
        *state_got,
        recv,
    )
    return (combined, new_weight[None], new_one[None], new_two[None])


def solution(mesh):
    return jax.shard_map(
        shards,
        mesh=mesh,
        in_specs=(
            P("expert", None, "dp"),
            P("expert", None),
            P("expert", None),
            P("expert", "dp"),
            P("expert", "dp", None),
            P("expert", "dp", None),
            P("expert", "dp", None),
            P(),
            P(),
        ),
        out_specs=(
            P("expert", "dp"),
            P("expert", "dp", None),
            P("expert", "dp", None),
            P("expert", "dp", None),
        ),
        check_vma=False,
    )
```

```python
import jax
import jax.numpy as jnp
from jax import lax
from jax.experimental import pallas as pl
from jax.experimental.pallas import tpu as pltpu
from jax.sharding import PartitionSpec as P

beta_one = 0.9
beta_two = 0.95
adam_eps = 1e-08
learn_rate = 0.001
weight_decay = 0.1
bias_one = 1.0 - 0.9**50 * 0.9**50
bias_two = 1.0 - 0.95**50 * 0.95**50

RING = 4
OLD_FAR = 3 * RING // 4
NEAR = [[far * RING + near for near in range(RING)] for far in range(RING)]
FAR = [[far * RING + near for far in range(RING)] for near in range(RING)]

LANES = 128
CHUNKS = 8
ROWS = 16

VMEM_BYTES = 48 * 1024 * 1024
PACK_VMEM_BYTES = 60 * 1024 * 1024
CONTRACT_LAST = (((1,), (1,)), ((), ()))
CONTRACT_FIRST = (((0,), (0,)), ((), ()))


def dot(left, right, dims=(((1,), (0,)), ((), ()))):
    return lax.dot_general(left, right, dims, preferred_element_type=jnp.float32)


def whole():
    return pl.BlockSpec(memory_space=pltpu.VMEM)


def gather_far(piece):
    return lax.all_gather(piece, "dp", axis=0, axis_index_groups=FAR)


def gather_near(piece):
    return lax.all_gather(piece, "dp", axis=0, axis_index_groups=NEAR)


def send_far(piece, step):
    pairs = [
        (far * RING + near, (far + step) % RING * RING + near)
        for far in range(OLD_FAR)
        for near in range(RING)
    ]
    return lax.ppermute(piece, "dp", pairs)


def iota(shape, axis):
    return lax.broadcasted_iota(jnp.int32, shape, axis)


def to_row(column):
    size = column.shape[0]
    same = iota((size, size), 0) == iota((size, size), 1)
    return jnp.sum(jnp.where(same, column, 0), axis=0, keepdims=True)


def pick(blocks_ref, wanted, first=0):
    near, far, every, tokens = blocks_ref.shape
    width = every - first
    column = iota((wanted.shape[0], width), 1)
    total = jnp.zeros((wanted.shape[0], tokens), jnp.float32)
    for x in range(near):
        for z in range(far):
            hot = (column + (z * near + x) * width == wanted).astype(jnp.bfloat16)
            total += dot(hot, blocks_ref[x, z, first:, :])
    return total


def slot_hot(slot_ref, slots):
    top, tokens = slot_ref.shape
    here = iota((slots, tokens), 0)
    return jnp.concatenate(
        [(here == slot_ref[k : k + 1, :]).astype(jnp.bfloat16) for k in range(top)], axis=1
    )


def dispatch_kernel(acts_ref, ids_ref, packed_ref, slot_ref):
    experts, half, wide = packed_ref.shape
    top, tokens = ids_ref.shape
    piece, cap = wide // 2, 2 * half
    every = top * tokens
    choices = jnp.concatenate([ids_ref[k : k + 1, :] for k in range(top)], axis=1)
    named = iota((experts, every), 0) == choices
    ahead = (iota((every, every), 0) < iota((every, every), 1)).astype(jnp.bfloat16)
    rank = dot(named.astype(jnp.bfloat16), ahead)
    rank = jnp.sum(jnp.where(named, rank, 0.0), axis=0, keepdims=True).astype(jnp.int32)
    slot = choices * cap + rank
    for k in range(top):
        slot_ref[k : k + 1, :] = slot[:, k * tokens : (k + 1) * tokens]
    features = jnp.concatenate(
        [acts_ref[k * piece : (k + 1) * piece, :] for k in range(top)], axis=1
    )
    row = iota((experts * half, every), 0)
    row = row // half * cap + row % half
    sides = [
        dot((row + side * half == slot).astype(jnp.bfloat16), features, CONTRACT_LAST)
        for side in range(2)
    ]
    packed = jnp.concatenate(sides, axis=1).astype(jnp.bfloat16)
    packed_ref[...] = packed.reshape(packed_ref.shape)


def scale_kernel(blocks_ref, wanted_ref, gates_ref, slot_ref, packed_ref):
    experts, lines, lanes = packed_ref.shape
    cap, width = lines // 2, wanted_ref.shape[0]
    top, tokens = gates_ref.shape
    chosen = pick(blocks_ref, wanted_ref[...], blocks_ref.shape[2] - width)
    scaled = jnp.concatenate(
        [(gates_ref[k : k + 1, :] * chosen).astype(jnp.bfloat16) for k in range(top)], axis=1
    )
    hot = slot_hot(slot_ref, experts * cap)
    short = 2 * lanes - width
    scaled = jnp.concatenate([scaled, jnp.zeros((short, top * tokens), jnp.bfloat16)], axis=0)
    packed = dot(hot, scaled, CONTRACT_LAST).astype(jnp.bfloat16)
    for c in range(2):
        packed_ref[:, c * cap : (c + 1) * cap, :] = packed[:, c * lanes : (c + 1) * lanes].reshape(
            experts, cap, lanes
        )


def tables(me, old_ref, new_ref, old_rows, width, cap):
    blocks, lanes = old_ref.shape
    far = me // RING
    leaving = jnp.zeros((old_rows, lanes), jnp.int32)
    origin = jnp.zeros((width, lanes), jnp.int32)
    model = jnp.zeros((width, lanes), jnp.int32)
    for i in range(blocks):
        old, new = old_ref[i : i + 1, :], new_ref[i : i + 1, :]
        number = iota((1, lanes), 1) + i * lanes
        leaving += jnp.where(old - me * old_rows == iota((old_rows, lanes), 0), new + 1, 0)
        row = iota((width, lanes), 0)
        held = new - me * width == row
        origin += jnp.where(held, old, 0)
        model += jnp.where(held, number, 0)
    leaving, origin, model = [
        jnp.sum(part, axis=1, keepdims=True) for part in (leaving, origin, model)
    ]
    mine = RING * width // lanes
    same = iota((lanes, lanes), 0) == iota((lanes, lanes), 1)
    own = jnp.concatenate(
        [
            jnp.sum(jnp.where(same, old_ref[pl.ds(far * mine + i, 1), :], 0), axis=1, keepdims=True)
            for i in range(mine)
        ],
        axis=0,
    )
    leaving_row = to_row(leaving)
    target, target_row = (leaving - 1) // width, (leaving_row - 1) // width
    size = (old_rows, old_rows)
    rank = jnp.sum(
        ((target == target_row) & (iota(size, 0) < iota(size, 1)) & (leaving > 0)).astype(jnp.int32),
        axis=0,
        keepdims=True,
    )
    step = (target_row // RING - far + RING) % RING
    send = (target_row % RING * RING + step) * cap + rank
    send = jnp.where(leaving_row > 0, send, -1)
    origin_row = to_row(origin)
    owner, owner_row = origin // old_rows, origin_row // old_rows
    rank = jnp.sum(
        ((owner == owner_row) & (origin_row < origin)).astype(jnp.int32), axis=1, keepdims=True
    )
    step = (far - owner // RING + RING) % RING
    recv = (step * RING + owner % RING) * cap + rank
    return send, recv, model, own


def pack_lines(source, slot, devices, cap):
    count = source.shape[0]
    rest = cap - ROWS
    lines = rest * CHUNKS
    index = iota((devices * ROWS, count), 0)
    hot = (index // ROWS * cap + index % ROWS == slot).astype(jnp.bfloat16)
    main = dot(hot, source)
    index = iota((devices * lines, count), 0)
    hot = (index // lines * cap + ROWS + index % rest == slot).astype(jnp.bfloat16)
    tail_rows = dot(hot, source)
    line = iota((devices * lines, LANES), 0) % lines // rest
    tail = jnp.zeros((devices * lines, LANES), jnp.float32)
    for c in range(CHUNKS):
        tail = jnp.where(line == c, tail_rows[:, c * LANES : (c + 1) * LANES], tail)
    mains = [main[:, c * LANES : (c + 1) * LANES].reshape(devices, ROWS, LANES) for c in range(CHUNKS)]
    return mains, tail.reshape(devices, lines, LANES)


def pack_kernel(me_ref, old_ref, new_ref, *refs):
    sources, (out_ref, recv_ref, model_ref, own_ref, held, sems) = refs[:3], refs[3:]
    copies = [pltpu.make_async_copy(source, held.at[i], sems.at[i]) for i, source in enumerate(sources)]
    for copy in copies:
        copy.start()
    devices, lines, _ = out_ref.shape
    cap = lines // (CHUNKS * len(sources))
    send, recv_ref[...], model_ref[...], own_ref[...] = tables(
        me_ref[0], old_ref, new_ref, held.shape[1], recv_ref.shape[0], cap
    )
    for copy in copies:
        copy.wait()
    place, tails = 0, []
    for number in range(len(sources)):
        mains, tail = pack_lines(held[number], send, devices, cap)
        for main in mains:
            out_ref[:, place : place + ROWS, :] = main.astype(jnp.bfloat16)
            place += ROWS
        tails.append(tail)
    out_ref[:, place:, :] = jnp.concatenate(tails, axis=1).astype(jnp.bfloat16)


class Arrived:
    def __init__(self, refs, recv, count):
        devices = sum(ref.shape[0] for ref in refs)
        lines = refs[0].shape[1]
        cap = lines // (CHUNKS * count)
        self.refs = refs
        width = recv.shape[0]
        rest = cap - ROWS
        self.lines = rest * CHUNKS
        index = iota((width, devices * ROWS), 1)
        self.main = (index // ROWS * cap + index % ROWS == recv).astype(jnp.bfloat16)
        index = iota((width, devices * self.lines), 1)
        self.tail = (index // self.lines * cap + ROWS + index % rest == recv).astype(jnp.bfloat16)
        self.chunk = iota((devices * self.lines, LANES), 0) % self.lines // rest
        start = count * CHUNKS * ROWS
        self.rest = jnp.concatenate([ref[:, start:, :].astype(jnp.float32) for ref in refs], axis=0)

    def piece(self, number, c):
        first = (number * CHUNKS + c) * ROWS
        rows = [ref[:, first : first + ROWS, :].reshape(-1, LANES) for ref in self.refs]
        rest = self.rest[:, number * self.lines : (number + 1) * self.lines, :].reshape(-1, LANES)
        rest = jnp.where(self.chunk == c, rest, 0.0).astype(jnp.bfloat16)
        return dot(self.main, jnp.concatenate(rows, axis=0)) + dot(self.tail, rest)


def forward_kernel(acts_ref, weight_ref, scaled_ref, rows_ref, out_ref):
    near, far, _, lanes = acts_ref.shape
    rows = rows_ref.shape[1]
    half = lanes // 2
    source, target = iota((2 * lanes, lanes), 0), iota((2 * lanes, lanes), 1)
    picked = jnp.where(target < half, target, target + half)
    shuffles = [(source == picked + side * half).astype(jnp.bfloat16) for side in range(2)]
    for z in range(far):
        for x in range(0, near, 2):
            pair = jnp.concatenate([acts_ref[x, z, :rows, :], acts_ref[x + 1, z, :rows, :]], axis=1)
            first = (z * near + x) * half
            for side in range(2):
                rows_ref[side, :, first : first + lanes] = dot(pair, shuffles[side]).astype(
                    jnp.bfloat16
                )
    blocks, lines, _ = scaled_ref.shape
    part = lines // 4
    out_ref[:, 5 * part :, :] = scaled_ref[...]
    columns, hidden = weight_ref.shape
    short = 5 * lanes // 2 - columns
    weight = jnp.concatenate([weight_ref[...], jnp.zeros((short, hidden), jnp.bfloat16)], axis=0)
    last = []
    for side in range(2):
        result = dot(rows_ref[side], weight, CONTRACT_LAST).astype(jnp.bfloat16)
        for c in range(2):
            first = (2 * c + side) * part
            out_ref[:, first : first + part, :] = result[:, c * lanes : (c + 1) * lanes].reshape(
                blocks, part, lanes
            )
        last.append(result[:, 2 * lanes :])
    out_ref[:, 4 * part : 5 * part, :] = jnp.concatenate(last, axis=1).reshape(blocks, part, lanes)


def combine_kernel(returned_ref, gates_ref, slot_ref, out_ref):
    experts, lines, lanes = returned_ref.shape
    part = lines // 9
    top, tokens = gates_ref.shape
    hot = slot_hot(slot_ref, experts * 2 * part).reshape(experts, 2 * part, top * tokens)
    each = [0.0, 0.0, 0.0]
    for side in range(2):
        mine = hot[:, side * part : (side + 1) * part, :].reshape(experts * part, top * tokens)
        for c in range(3):
            first = (2 * c + side) * part if c < 2 else 4 * part
            rows = returned_ref[:, first : first + part, :].reshape(experts * part, lanes)
            if c == 2:
                rows = rows[:, side * (lanes // 2) : (side + 1) * (lanes // 2)]
            each[c] += dot(rows, mine, CONTRACT_FIRST)
    first = 0
    for piece in each:
        total = jnp.zeros((piece.shape[0], tokens), jnp.float32)
        for k in range(top):
            total += gates_ref[k : k + 1, :] * piece[:, k * tokens : (k + 1) * tokens]
        count = min(piece.shape[0], out_ref.shape[0] - first)
        out_ref[first : first + count, :] = total[:count].astype(jnp.bfloat16)
        first += count


def spread_kernel(me_ref, blocks_ref, own_ref, out_ref):
    far, width, tokens = blocks_ref.shape
    far = OLD_FAR
    near = me_ref[0] % RING
    column = iota((own_ref.shape[0], far * width), 1)
    column = (column // width * RING + near) * width + column % width
    hot = (column == own_ref[...]).astype(jnp.bfloat16)
    rows = dot(hot, blocks_ref[:far].reshape(far * width, tokens))
    out_ref[...] = rows.astype(jnp.bfloat16).reshape(out_ref.shape)


def sum_kernel(parts_ref, out_ref):
    out_ref[...] = jnp.sum(parts_ref[...].astype(jnp.float32), axis=0).astype(jnp.bfloat16)


def update_kernel(rows_ref, returned_ref, *refs):
    recv_ref, w_ref, m_ref, v_ref = refs[RING:]
    blocks, lines, lanes = returned_ref.shape
    part = lines // 9
    total = 0.0
    for side in range(2):
        scaled = [
            returned_ref[:, (5 + 2 * c + side) * part : (6 + 2 * c + side) * part, :].reshape(
                blocks * part, lanes
            )
            for c in range(2)
        ]
        total += dot(jnp.concatenate(scaled, axis=1), rows_ref[side], CONTRACT_FIRST)
    total = total[: w_ref.shape[0]]
    arrived = Arrived(refs[:RING], recv_ref[...], 3)
    for c in range(CHUNKS):
        piece = slice(c * LANES, (c + 1) * LANES)
        gradient = total[:, piece]
        weight = arrived.piece(0, c)
        one_next = beta_one * arrived.piece(1, c) + (1.0 - beta_one) * gradient
        two_next = beta_two * arrived.piece(2, c) + (1.0 - beta_two) * gradient * gradient
        update = (
            one_next / bias_one / (jnp.sqrt(two_next / bias_two) + adam_eps)
            + weight_decay * weight
        )
        w_ref[:, piece] = (weight - learn_rate * update).astype(jnp.bfloat16)
        m_ref[:, piece] = one_next.astype(jnp.bfloat16)
        v_ref[:, piece] = two_next.astype(jnp.bfloat16)


def call(kernel, name, out_shape, *args, flops=0, scalars=0, apart=(), scratch=(), order=(), vmem=VMEM_BYTES):
    several = isinstance(out_shape, tuple)
    count = len(args)

    def body(*refs):
        kernel(*refs[:count], *refs[count + len(order) :])

    specs = [pl.BlockSpec(memory_space=pltpu.SMEM)] * scalars + [whole()] * (count - scalars)
    for i in apart:
        specs[i] = pl.BlockSpec(memory_space=pltpu.HBM)
    return pl.pallas_call(
        body,
        out_shape=out_shape,
        in_specs=specs + [pl.BlockSpec(memory_space=pl.ANY)] * len(order),
        out_specs=tuple(whole() for _ in out_shape) if several else whole(),
        scratch_shapes=scratch,
        compiler_params=pltpu.CompilerParams(vmem_limit_bytes=vmem),
        cost_estimate=pl.CostEstimate(flops=flops, bytes_accessed=1024, transcendentals=0),
        name=name,
    )(*args, *order)


def shards(
    hidden_acts,
    expert_ids,
    gate_weights,
    cotangent,
    weight_old,
    first_old,
    second_old,
    old_place,
    new_place,
):
    n_expert = lax.axis_size("expert")
    n_data = lax.axis_size("dp")
    me = lax.axis_index("dp")
    tok_rows, top_count, piece = hidden_acts.shape
    hidden = weight_old.shape[2]
    width = cotangent.shape[1]
    old_group = 3 * n_data // 4
    move_cap = (width + old_group - 1) // old_group
    cap = 2 * tok_rows * top_count // n_expert
    slots = n_expert * cap
    int32 = jnp.int32

    def shape(*sizes, dtype=jnp.bfloat16):
        return jax.ShapeDtypeStruct(sizes, dtype)

    def exchange(array, axis, groups=None):
        return lax.all_to_all(
            array, axis, split_axis=0, concat_axis=0, tiled=True, axis_index_groups=groups
        )

    rows = slots // 2
    packed, slot = call(
        dispatch_kernel,
        "dispatch",
        (shape(n_expert, cap // 2, 2 * piece), shape(top_count, tok_rows, dtype=int32)),
        hidden_acts.transpose(1, 2, 0).reshape(top_count * piece, tok_rows),
        expert_ids.T,
    )
    arrived = exchange(packed, "expert")

    device = me[None].astype(int32)
    lines = hidden // LANES * move_cap
    old_rows = weight_old.shape[1]
    column = shape(width, 1, dtype=int32)
    sent, recv, model, own = call(
        pack_kernel,
        "pack",
        (
            shape(n_data, 3 * lines, LANES),
            column,
            column,
            shape(RING * width, 1, dtype=int32),
        ),
        device,
        old_place.reshape(-1, LANES),
        new_place.reshape(-1, LANES),
        weight_old[0],
        first_old[0],
        second_old[0],
        scalars=1,
        vmem=PACK_VMEM_BYTES,
        apart=(3, 4, 5),
        scratch=[pltpu.VMEM((3, old_rows, hidden), jnp.bfloat16), pltpu.SemaphoreType.DMA((3,))],
    )
    sent, arrived = lax.optimization_barrier((sent, arrived))
    state = exchange(sent.reshape(RING, RING, 3 * lines, LANES), "dp", NEAR)

    both = jnp.concatenate([arrived.reshape(rows, 2 * piece), cotangent.T], axis=0)
    both_far, state = lax.optimization_barrier((gather_far(both), state))
    both_all = gather_near(both_far)
    gates = gate_weights.T

    scaled = call(
        scale_kernel, "scale", shape(n_expert, 2 * cap, LANES), both_all, model, gates, slot
    )

    state_got = [send_far(state[:, step], step) if step else state[:, 0] for step in range(RING)]

    def tail(forward_name):
        def run(both_all, weight, scaled, slot, gates):
            rows_now, outputs = call(
                forward_kernel,
                forward_name,
                (shape(2, rows, hidden), shape(n_expert, 9 * cap // 2, LANES)),
                both_all,
                weight,
                scaled,
            )
            returned = exchange(outputs, "expert")
            part = call(combine_kernel, "combine", shape(old_rows, tok_rows), returned, gates, slot)
            return rows_now, part, returned

        return run

    rows_now, part, returned = lax.cond(
        new_place[0] >= 0,
        tail("forward"),
        tail("forward_too"),
        both_all,
        weight_old[0],
        scaled,
        slot,
        gates,
    )
    part, state_got = lax.optimization_barrier((part, state_got))
    spread = call(
        spread_kernel,
        "spread",
        shape(RING, width, tok_rows),
        device,
        gather_far(part),
        own,
        scalars=1,
    )
    combined = call(sum_kernel, "sum", shape(width, tok_rows), exchange(spread, "dp", NEAR)).T
    new_weight, new_one, new_two = call(
        update_kernel,
        "update",
        (shape(width, hidden),) * 3,
        rows_now,
        returned,
        *state_got,
        recv,
    )
    return (combined, new_weight[None], new_one[None], new_two[None])


def solution(mesh):
    return jax.shard_map(
        shards,
        mesh=mesh,
        in_specs=(
            P("expert", None, "dp"),
            P("expert", None),
            P("expert", None),
            P("expert", "dp"),
            P("expert", "dp", None),
            P("expert", "dp", None),
            P("expert", "dp", None),
            P(),
            P(),
        ),
        out_specs=(
            P("expert", "dp"),
            P("expert", "dp", None),
            P("expert", "dp", None),
            P("expert", "dp", None),
        ),
        check_vma=False,
    )
```
